1024 devices in a mesh: mx: 64 (over x, y), my: 16 (over z, core).
Axes of the slice: x: 8, y: 8, z: 8, core: 2. Of those that a mesh axis runs over, the one named last changes fastest.
Arguments:
- tokens: bfloat16 [2048, 18432], P('mx', 'my'), may hold values from -6 to 6
- q_weight: bfloat16 [18432, 12288], P('my', 'mx'), may hold values from -0.046875 to 0.046875
- kv_weight: bfloat16 [18432, 512], P('my'), may hold values from -0.046875 to 0.046875
- key_cache: bfloat16 [2048, 1024, 256], P(('mx', 'my')), may hold values from -450 to 450
- value_cache: bfloat16 [2048, 1024, 256], P(('mx', 'my')), may hold values from -6 to 6
- lengths: int32 [2048], P(('mx', 'my')), may hold values from 1 to 1024, 1048576 in all
Outputs:
- attended: bfloat16 [2048, 12288], P(('mx', 'my'))
The draws below stay inside these ranges and needn't reach their ends.
Inputs may be any that keep to these rules, and one draw needn't show every extreme that they name: lengths[r] slots of row r hold cached tokens; some row has all 1024.
All inputs are finite; a program needn't handle non-finite values. No bound on the sum of `lengths` on one device may be relied on, other than what follows from the above.
Results may differ from the reference program's by a relative error of at most 0.022.
Values may be sent and summed in bfloat16 or wider, within the bound.
No kernel may reach another device: no remote copies, remote signals or barrier semaphores. Data moves between devices by JAX's collectives and lax.ppermute only.
A program may use at most 32 MiB of HBM per device.

```python
import math
import jax
import jax.numpy as jnp
import numpy as np
from jax import lax

D = 18432
HEADS = 48
HD = 256
CTX = 1024
ROWS = 2048


def draw_key_cache(key, part):
    key = jax.random.fold_in(key, 7)
    base_key = jax.random.fold_in(key, 0)
    full_shape = (ROWS, CTX, HD)
    values = jax.random.truncated_normal(base_key, -6.0, 6.0, full_shape, jnp.float32)
    return values.astype(jnp.bfloat16)


def level_of(own_key, extent, cuts, low, high):
    level = 1.0
    for axis_at, parts in cuts:
        draws = jax.random.uniform(jax.random.fold_in(jax.random.fold_in(own_key, 6), axis_at), (parts,), jnp.float32, low / len(cuts), high / len(cuts))
        level = level * jnp.repeat(jnp.exp(draws), extent[axis_at] // parts).reshape((-1,) + (1,) * (len(extent) - 1 - axis_at))
    return level


def length_profile(count, total, limit, skew):
    portions = [(1 << 20) // math.isqrt(grade ** skew) + 1 for grade in range(2, count + 1)]
    surplus, holding = total - limit - (count - 1), [1] * (count - 1)
    while surplus > 0:
        candidates = [i for i in range(count - 1) if holding[i] < limit]
        whole, budget = sum([portions[i] for i in candidates]), surplus
        for i in candidates:
            more = min(limit - holding[i], max(1, budget * portions[i] // whole), surplus)
            holding[i] = holding[i] + more
            surplus = surplus - more
    return np.array([limit] + holding)


def ragged_sizes(own_key, number_of, total, most, lean):
    if number_of == 2:
        one = jax.random.randint(own_key, (), max(1, total - most), min(most, total - 1) + 1)
        return jnp.stack([one, total - one])
    sizes = jnp.asarray(length_profile(number_of, total, most, lean), jnp.int32)
    pairs = (number_of - 1) // 2
    source_of, sink = sizes[1:1 + 2 * pairs:2], sizes[2:2 + 2 * pairs:2]
    slack = jnp.minimum(source_of - 1, most - sink)
    passed = jax.random.randint(jax.random.fold_in(own_key, 1), (pairs,), 0, 1 << 20) % (slack + 1)
    sizes = sizes.at[1:1 + 2 * pairs:2].set(source_of - passed).at[2:2 + 2 * pairs:2].set(sink + passed)
    return sizes[jax.random.permutation(jax.random.fold_in(own_key, 2), number_of)]


def gaussian(rng, dims, scale, reach, cuts=(), dtype=jnp.bfloat16):
    level = level_of(rng, dims, cuts, -0.22, 0.18) if cuts else 1.0
    drawn = jax.random.normal(rng, dims, jnp.float32) * scale * level
    return jnp.minimum(jnp.maximum(drawn, -reach), reach).astype(dtype)


def setup_inputs(seed: int = 0) -> dict:
    arg_keys = jax.random.split(jax.random.key(seed), 7)
    tokens = gaussian(arg_keys[0], (ROWS, D), 1.0, 6.0, ((0, 64), (1, 16)))
    q_weight = gaussian(arg_keys[1], (D, HEADS * HD), D ** -0.5, 0.046875, ((0, 16), (1, 64)))
    kv_weight = gaussian(arg_keys[2], (D, 2 * HD), D ** -0.5, 0.046875, ((0, 16),))
    key_cache = draw_key_cache(jax.random.fold_in(arg_keys[6], 71), 0)
    value_cache = gaussian(arg_keys[4], (ROWS, CTX, HD), 1.0, 6.0, ((0, 1024),))
    lengths = ragged_sizes(arg_keys[5], ROWS, ROWS * CTX // 2, CTX, 1).astype(jnp.int32)
    return dict(tokens=tokens, q_weight=q_weight, kv_weight=kv_weight, key_cache=key_cache, value_cache=value_cache, lengths=lengths)


def attend(pieces_in):
    query_block, key_block, value_block, new_key, new_value, row_lengths = pieces_in
    scale_factor = 1.0 / math.sqrt(HD)
    query_float = query_block.astype(jnp.float32)
    scores = jnp.einsum('rhd,rcd->rhc', query_float, key_block.astype(jnp.float32)) * scale_factor
    own_score = jnp.einsum('rhd,rd->rh', query_float, new_key.astype(jnp.float32)) * scale_factor
    live_mask = jnp.arange(CTX)[None, None, :] < row_lengths[:, None, None]
    peak_score = jnp.maximum(lax.optimization_barrier(jnp.max(jnp.where(live_mask, scores, -jnp.inf), axis=2)), own_score)
    raw_weights = jnp.where(live_mask, jnp.exp(scores - peak_score[:, :, None]), 0.0)
    own_raw = jnp.exp(own_score - peak_score)
    totals = lax.optimization_barrier(jnp.sum(raw_weights, axis=2)) + own_raw
    weights = (raw_weights / totals[:, :, None]).astype(jnp.bfloat16)
    own_weight = (own_raw / totals).astype(jnp.bfloat16)
    blended = jnp.einsum('rhc,rcd->rhd', weights.astype(jnp.float32), value_block.astype(jnp.float32))
    blended = blended + own_weight.astype(jnp.float32)[:, :, None] * new_value.astype(jnp.float32)[:, None, :]
    return blended.astype(jnp.bfloat16)

def reference(tokens, q_weight, kv_weight, key_cache, value_cache, lengths):
    queries = jnp.dot(tokens, q_weight, preferred_element_type=jnp.float32).astype(jnp.bfloat16)
    new_pairs = jnp.dot(tokens, kv_weight, preferred_element_type=jnp.float32).astype(jnp.bfloat16)
    block_rows = math.gcd(ROWS, 64)
    block_count = ROWS // block_rows
    query_blocks = queries.reshape(block_count, block_rows, HEADS, HD)
    key_blocks = key_cache.reshape(block_count, block_rows, CTX, HD)
    value_blocks = value_cache.reshape(block_count, block_rows, CTX, HD)
    new_keys = new_pairs[:, :HD].reshape(block_count, block_rows, HD)
    new_values = new_pairs[:, HD:].reshape(block_count, block_rows, HD)
    length_blocks = lengths.reshape(block_count, block_rows)
    attended = lax.map(attend, (query_blocks, key_blocks, value_blocks, new_keys, new_values, length_blocks))
    return attended.reshape(ROWS, HEADS * HD)
```

```python
import math

import jax
import jax.numpy as jnp
from jax import lax
from jax.sharding import PartitionSpec as P

SIDE = 8
HALF = SIDE // 2


def shift_y(step):
    return [
        (SIDE * x + y, SIDE * x + (y + step) % SIDE) for x in range(SIDE) for y in range(SIDE)
    ]


def local(tokens, q_weight, kv_weight, key_cache, value_cache, lengths):
    my_count = lax.axis_size("my")
    planes = my_count // 2
    own_rows = tokens.shape[0] // my_count
    width = tokens.shape[1]
    columns = q_weight.shape[1]
    half_columns = columns // 2
    head_size = key_cache.shape[2]
    slot_count = key_cache.shape[1]
    y_index = lax.axis_index("mx") % SIDE
    core = lax.axis_index("my") % 2

    ordered = tokens.reshape(planes, 2, own_rows, width).transpose(1, 0, 2, 3)
    ordered = ordered.reshape(-1, width)
    across = lax.ppermute(ordered, "mx", shift_y(HALF))
    lower = y_index < HALF
    pair = jnp.stack([jnp.where(lower, ordered, across), jnp.where(lower, across, ordered)])
    x_rings = [[SIDE * x + y for x in range(SIDE)] for y in range(SIDE)]
    gathered = lax.all_gather(pair, "mx", axis=0, tiled=True, axis_index_groups=x_rings)

    from_below = lax.ppermute(q_weight, "mx", shift_y(1))
    from_above = lax.ppermute(q_weight, "mx", shift_y(-1))
    from_two_below = lax.ppermute(q_weight[:, half_columns:], "mx", shift_y(2))
    from_two_above = lax.ppermute(q_weight[:, :half_columns], "mx", shift_y(-2))
    weights_here = jnp.concatenate(
        [from_two_below, from_below, q_weight, from_above, from_two_above], axis=1
    )

    new_partial = jnp.dot(tokens, kv_weight, preferred_element_type=jnp.float32)
    new_parts = lax.all_to_all(
        new_partial.reshape(my_count, own_rows, -1), "my", split_axis=0, concat_axis=0
    )
    new_pairs = jnp.sum(new_parts, axis=0).astype(jnp.bfloat16)

    gathered = gathered.reshape(2 * SIDE, 2, planes, own_rows, width).transpose(1, 2, 0, 3, 4)
    gathered = gathered.reshape(2, -1, width)
    other_rows = lax.dynamic_index_in_dim(gathered, 1 - core, 0, keepdims=False)
    same_rows = lax.dynamic_index_in_dim(gathered, core, 0, keepdims=False)
    other_sums = jnp.dot(other_rows, weights_here, preferred_element_type=jnp.float32)
    swapped = lax.ppermute(other_sums, "my", [(i, i ^ 1) for i in range(my_count)])
    same_sums = jnp.dot(same_rows, weights_here, preferred_element_type=jnp.float32)
    chip_sums = (same_sums + swapped).reshape(planes, -1, 4 * columns)

    plane_groups = [[2 * plane + one for plane in range(planes)] for one in range(2)]
    plane_parts = lax.all_to_all(
        chip_sums, "my", split_axis=0, concat_axis=0, axis_index_groups=plane_groups
    )
    query_block = jnp.sum(plane_parts, axis=0).astype(jnp.bfloat16)

    row_groups = [
        [SIDE * x + y + HALF * upper for x in range(SIDE) for upper in range(2)]
        for y in range(HALF)
    ]
    query_rows = lax.all_to_all(
        query_block.reshape(2 * SIDE, own_rows, -1),
        "mx",
        split_axis=0,
        concat_axis=0,
        axis_index_groups=row_groups,
    )
    strip = SIDE * columns
    query_rows = query_rows.reshape(SIDE, 2, own_rows, 4 * columns).transpose(2, 0, 1, 3)
    query_rows = query_rows.reshape(own_rows, SIDE, strip)
    color = y_index % HALF
    turned = [
        jnp.roll(query_rows, (one - 2) * columns + half_columns, axis=2) for one in range(HALF)
    ]
    queries = lax.select_n(
        jnp.broadcast_to(color, query_rows.shape), *turned
    ).reshape(own_rows, -1, head_size)

    new_key = new_pairs[:, :head_size]
    new_value = new_pairs[:, head_size:]
    scale_factor = 1.0 / math.sqrt(head_size)
    scores = (
        jnp.einsum("rhd,rcd->rhc", queries, key_cache, preferred_element_type=jnp.float32)
        * scale_factor
    )
    own_score = (
        jnp.einsum("rhd,rd->rh", queries, new_key, preferred_element_type=jnp.float32)
        * scale_factor
    )
    slot_index = lax.broadcasted_iota(jnp.int32, (1, 1, slot_count), 2)
    live_mask = slot_index < lengths[:, None, None]
    peak_score = jnp.maximum(jnp.max(jnp.where(live_mask, scores, -jnp.inf), axis=2), own_score)
    raw_weights = jnp.where(live_mask, jnp.exp(scores - peak_score[:, :, None]), 0.0)
    own_raw = jnp.exp(own_score - peak_score)
    totals = jnp.sum(raw_weights, axis=2) + own_raw
    weights = (raw_weights / totals[:, :, None]).astype(jnp.bfloat16)
    own_weight = (own_raw / totals).astype(jnp.bfloat16)
    blended = jnp.einsum("rhc,rcd->rhd", weights, value_cache, preferred_element_type=jnp.float32)
    blended = (
        blended
        + own_weight.astype(jnp.float32)[:, :, None] * new_value.astype(jnp.float32)[:, None, :]
    )
    return blended.astype(jnp.bfloat16).reshape(own_rows, -1)


def solution(mesh):
    return jax.shard_map(
        local,
        mesh=mesh,
        in_specs=(
            P("mx", "my"),
            P("my", "mx"),
            P("my", None),
            P(("mx", "my"), None, None),
            P(("mx", "my"), None, None),
            P(("mx", "my")),
        ),
        out_specs=P(("mx", "my"), None),
        check_vma=False,
    )
```

```python
import math

import jax
import jax.numpy as jnp
from jax import lax
from jax.sharding import PartitionSpec as P

SIDE = 8


def local(tokens, q_weight, kv_weight, key_cache, value_cache, lengths):
    my_count = lax.axis_size("my")
    planes = my_count // 2
    own_rows = tokens.shape[0] // my_count
    width = tokens.shape[1]
    head_size = key_cache.shape[2]
    slot_count = key_cache.shape[1]
    core = lax.axis_index("my") % 2

    x_rings = [[SIDE * x + y for x in range(SIDE)] for y in range(SIDE)]
    y_rings = [[SIDE * x + y for y in range(SIDE)] for x in range(SIDE)]
    weights_here = lax.all_gather(q_weight, "mx", axis=1, tiled=True, axis_index_groups=y_rings)
    gathered = lax.all_gather(tokens, "mx", axis=0, tiled=True, axis_index_groups=x_rings)

    tokens, gathered = lax.optimization_barrier((tokens, gathered))
    new_partial = jnp.dot(tokens, kv_weight, preferred_element_type=jnp.float32)
    new_parts = lax.all_to_all(
        new_partial.reshape(my_count, own_rows, -1), "my", split_axis=0, concat_axis=0
    )
    new_pairs = jnp.sum(new_parts, axis=0).astype(jnp.bfloat16)

    gathered = gathered.reshape(SIDE, planes, 2, own_rows, width).transpose(2, 1, 0, 3, 4)
    gathered = gathered.reshape(2, -1, width)
    other_rows = lax.dynamic_index_in_dim(gathered, 1 - core, 0, keepdims=False)
    same_rows = lax.dynamic_index_in_dim(gathered, core, 0, keepdims=False)
    other_rows, same_rows, new_pairs = lax.optimization_barrier(
        (other_rows, same_rows, new_pairs)
    )
    other_sums = jnp.dot(other_rows, weights_here, preferred_element_type=jnp.float32)
    swapped = lax.ppermute(other_sums, "my", [(i, i ^ 1) for i in range(my_count)])
    same_sums = jnp.dot(same_rows, weights_here, preferred_element_type=jnp.float32)
    chip_sums = (same_sums + swapped).reshape(planes * SIDE, own_rows, -1)

    groups = [
        [(SIDE * x + y) * my_count + 2 * plane + one for plane in range(planes) for x in range(SIDE)]
        for y in range(SIDE)
        for one in range(2)
    ]
    parts = lax.all_to_all(
        chip_sums, ("mx", "my"), split_axis=0, concat_axis=0, axis_index_groups=groups
    )
    query_rows = jnp.sum(parts.reshape(planes, SIDE, own_rows, -1), axis=0).astype(jnp.bfloat16)
    queries = query_rows.transpose(1, 0, 2).reshape(own_rows, -1, head_size)

    new_key = new_pairs[:, :head_size]
    new_value = new_pairs[:, head_size:]
    scale_factor = 1.0 / math.sqrt(head_size)
    scores = (
        jnp.einsum("rhd,rcd->rhc", queries, key_cache, preferred_element_type=jnp.float32)
        * scale_factor
    )
    own_score = (
        jnp.einsum("rhd,rd->rh", queries, new_key, preferred_element_type=jnp.float32)
        * scale_factor
    )
    slot_index = lax.broadcasted_iota(jnp.int32, (1, 1, slot_count), 2)
    live_mask = slot_index < lengths[:, None, None]
    peak_score = jnp.maximum(jnp.max(jnp.where(live_mask, scores, -jnp.inf), axis=2), own_score)
    raw_weights = jnp.where(live_mask, jnp.exp(scores - peak_score[:, :, None]), 0.0)
    own_raw = jnp.exp(own_score - peak_score)
    totals = jnp.sum(raw_weights, axis=2) + own_raw
    weights = (raw_weights / totals[:, :, None]).astype(jnp.bfloat16)
    own_weight = (own_raw / totals).astype(jnp.bfloat16)
    blended = jnp.einsum("rhc,rcd->rhd", weights, value_cache, preferred_element_type=jnp.float32)
    blended = (
        blended
        + own_weight.astype(jnp.float32)[:, :, None] * new_value.astype(jnp.float32)[:, None, :]
    )
    return blended.astype(jnp.bfloat16).reshape(own_rows, -1)


def solution(mesh):
    return jax.shard_map(
        local,
        mesh=mesh,
        in_specs=(
            P("mx", "my"),
            P("my", "mx"),
            P("my", None),
            P(("mx", "my"), None, None),
            P(("mx", "my"), None, None),
            P(("mx", "my")),
        ),
        out_specs=P(("mx", "my"), None),
        check_vma=False,
    )
```

```python
import functools
import math

import jax
import jax.numpy as jnp
from jax import lax
from jax.experimental import pallas as pl
from jax.experimental.pallas import tpu as pltpu
from jax.sharding import PartitionSpec as P

SIDE = 8
LANES = 128
TILE = 256


def project_body(blocks, rows_ref, weights_ref, other_ref, same_ref):
    half = rows_ref.shape[0] // 2
    sums = lax.dot_general(
        rows_ref[...],
        weights_ref[...],
        (((1,), (1,)), ((), ())),
        preferred_element_type=jnp.float32,
    )
    first = pl.program_id(0) * (TILE // LANES)
    for at in range(TILE // LANES):
        lanes = slice(at * LANES, (at + 1) * LANES)
        place = pl.ds(first + at, half, stride=blocks)
        other_ref[place, :] = sums[:half, lanes]
        same_ref[place, :] = sums[half:, lanes]


def project(rows, weights):
    half = rows.shape[0] // 2
    columns, width = weights.shape
    blocks = columns // LANES
    product = jax.ShapeDtypeStruct((half * blocks, LANES), jnp.float32)
    whole = pl.BlockSpec((half * blocks, LANES), lambda i: (0, 0))
    return pl.pallas_call(
        functools.partial(project_body, blocks),
        grid=(columns // TILE,),
        in_specs=[
            pl.BlockSpec(rows.shape, lambda i: (0, 0)),
            pl.BlockSpec((TILE, width), lambda i: (i, 0)),
        ],
        out_specs=[whole, whole],
        out_shape=[product, product],
        compiler_params=pltpu.CompilerParams(vmem_limit_bytes=58 * 2**20),
        cost_estimate=pl.CostEstimate(
            flops=2 * rows.size * columns,
            bytes_accessed=2 * (rows.size + weights.size) + 8 * half * columns,
            transcendentals=0,
        ),
        name="project",
    )(rows, weights)


def local(tokens, q_weight, kv_weight, key_cache, value_cache, lengths):
    my_count = lax.axis_size("my")
    planes = my_count // 2
    own_rows = tokens.shape[0] // my_count
    width = tokens.shape[1]
    head_size = key_cache.shape[2]
    slot_count = key_cache.shape[1]
    core = lax.axis_index("my") % 2

    x_rings = [[SIDE * x + y for x in range(SIDE)] for y in range(SIDE)]
    y_rings = [[SIDE * x + y for y in range(SIDE)] for x in range(SIDE)]
    weights_here = lax.all_gather(q_weight, "mx", axis=1, tiled=True, axis_index_groups=y_rings)
    gathered = lax.all_gather(tokens, "mx", axis=0, tiled=True, axis_index_groups=x_rings)

    tokens, gathered = lax.optimization_barrier((tokens, gathered))
    new_partial = jnp.dot(tokens, kv_weight, preferred_element_type=jnp.float32)
    new_parts = lax.all_to_all(
        new_partial.reshape(my_count, own_rows, -1), "my", split_axis=0, concat_axis=0
    )
    new_pairs = jnp.sum(new_parts, axis=0).astype(jnp.bfloat16)

    gathered = gathered.reshape(SIDE, planes, 2, own_rows, width).transpose(2, 1, 0, 3, 4)
    gathered = gathered.reshape(2, -1, width)
    other_rows = lax.dynamic_index_in_dim(gathered, 1 - core, 0, keepdims=False)
    same_rows = lax.dynamic_index_in_dim(gathered, core, 0, keepdims=False)
    both_rows = jnp.concatenate([other_rows, same_rows], axis=0)
    both_rows, new_pairs = lax.optimization_barrier((both_rows, new_pairs))
    other_sums, same_sums = project(both_rows, weights_here.T)
    swapped = lax.ppermute(other_sums, "my", [(i, i ^ 1) for i in range(my_count)])
    chip_sums = (same_sums + swapped).reshape(planes * SIDE, -1, LANES)

    groups = [
        [(SIDE * x + y) * my_count + 2 * plane + one for plane in range(planes) for x in range(SIDE)]
        for y in range(SIDE)
        for one in range(2)
    ]
    parts = lax.all_to_all(
        chip_sums, ("mx", "my"), split_axis=0, concat_axis=0, axis_index_groups=groups
    )
    query_rows = jnp.sum(parts.reshape(planes, SIDE, own_rows, -1, LANES), axis=0)
    query_rows = query_rows.astype(jnp.bfloat16).transpose(1, 0, 2, 3)
    queries = query_rows.reshape(own_rows, -1, head_size)

    new_key = new_pairs[:, :head_size]
    new_value = new_pairs[:, head_size:]
    scale_factor = 1.0 / math.sqrt(head_size)
    scores = (
        jnp.einsum("rhd,rcd->rhc", queries, key_cache, preferred_element_type=jnp.float32)
        * scale_factor
    )
    own_score = (
        jnp.einsum("rhd,rd->rh", queries, new_key, preferred_element_type=jnp.float32)
        * scale_factor
    )
    slot_index = lax.broadcasted_iota(jnp.int32, (1, 1, slot_count), 2)
    live_mask = slot_index < lengths[:, None, None]
    peak_score = jnp.maximum(jnp.max(jnp.where(live_mask, scores, -jnp.inf), axis=2), own_score)
    raw_weights = jnp.where(live_mask, jnp.exp(scores - peak_score[:, :, None]), 0.0)
    own_raw = jnp.exp(own_score - peak_score)
    totals = jnp.sum(raw_weights, axis=2) + own_raw
    weights = (raw_weights / totals[:, :, None]).astype(jnp.bfloat16)
    own_weight = (own_raw / totals).astype(jnp.bfloat16)
    blended = jnp.einsum("rhc,rcd->rhd", weights, value_cache, preferred_element_type=jnp.float32)
    blended = (
        blended
        + own_weight.astype(jnp.float32)[:, :, None] * new_value.astype(jnp.float32)[:, None, :]
    )
    return blended.astype(jnp.bfloat16).reshape(own_rows, -1)


def solution(mesh):
    return jax.shard_map(
        local,
        mesh=mesh,
        in_specs=(
            P("mx", "my"),
            P("my", "mx"),
            P("my", None),
            P(("mx", "my"), None, None),
            P(("mx", "my"), None, None),
            P(("mx", "my")),
        ),
        out_specs=P(("mx", "my"), None),
        check_vma=False,
    )
```

```python
import functools
import math

import jax
import jax.numpy as jnp
from jax import lax
from jax.experimental import pallas as pl
from jax.experimental.pallas import tpu as pltpu
from jax.sharding import PartitionSpec as P

SIDE = 8
LANES = 128
NEAR = 3
FAR = SIDE - NEAR


def times(rows, weights):
    return lax.dot_general(
        rows, weights, (((1,), (1,)), ((), ())), preferred_element_type=jnp.float32
    )


def near_body(rows_ref, below_ref, own_ref, above_ref, pair_ref, other_ref, same_ref, held):
    at = 0
    for piece in (below_ref, own_ref, above_ref, pair_ref):
        held[at : at + piece.shape[0], :] = piece[...]
        at += piece.shape[0]
    half = rows_ref.shape[0] // 2
    sums = times(rows_ref[...], held[...])
    other_ref[...] = sums[:half]
    same_ref[...] = sums[half:]


def near_sums(rows, *pieces):
    half, width = rows.shape[0] // 2, rows.shape[1]
    columns = sum(piece.shape[0] for piece in pieces)
    product = jax.ShapeDtypeStruct((half, columns), jnp.float32)
    return pl.pallas_call(
        near_body,
        out_shape=[product, product],
        scratch_shapes=[pltpu.VMEM((columns, width), jnp.bfloat16)],
        compiler_params=pltpu.CompilerParams(vmem_limit_bytes=16 * 2**20),
        cost_estimate=pl.CostEstimate(
            flops=4 * half * width * columns,
            bytes_accessed=2 * width * (2 * half + columns) + 8 * half * columns,
            transcendentals=0,
        ),
        name="near_sums",
    )(rows, *pieces)


def far_body(blocks, y_ref, rows_ref, weights_ref, other_ref, same_ref, held, sems):
    columns = weights_ref.shape[0] // SIDE
    half = rows_ref.shape[0] // 2
    copies = []
    for at in range(FAR):
        source = lax.rem(y_ref[0] + 2 + at, SIDE) * columns
        copies.append(
            pltpu.make_async_copy(
                weights_ref.at[pl.ds(pl.multiple_of(source, columns), columns), :],
                held.at[pl.ds(at * columns, columns), :],
                sems.at[at],
            )
        )
        copies[-1].start()
    rest = held.shape[0] - FAR * columns
    held[FAR * columns :, :] = jnp.zeros((rest, held.shape[1]), held.dtype)
    waited, done = 0, 0
    while done < blocks:
        last = min(done + 3, blocks)
        while waited < FAR and waited * columns < last * LANES:
            copies[waited].wait()
            waited += 1
        sums = times(rows_ref[...], held[done * LANES : last * LANES, :])
        for block in range(done, last):
            lanes = slice((block - done) * LANES, (block - done + 1) * LANES)
            place = pl.ds(block, half, stride=blocks)
            other_ref[place, :] = sums[:half, lanes]
            same_ref[place, :] = sums[half:, lanes]
        done = last


def far_sums(y_index, rows, weights):
    half, width = rows.shape[0] // 2, rows.shape[1]
    columns = weights.shape[0] // SIDE
    blocks = -(-FAR * columns // LANES)
    product = jax.ShapeDtypeStruct((half * blocks, LANES), jnp.float32)
    in_vmem = pl.BlockSpec(memory_space=pltpu.VMEM)
    return pl.pallas_call(
        functools.partial(far_body, blocks),
        in_specs=[
            pl.BlockSpec(memory_space=pltpu.SMEM),
            in_vmem,
            pl.BlockSpec(memory_space=pltpu.HBM),
        ],
        out_specs=[in_vmem, in_vmem],
        out_shape=[product, product],
        scratch_shapes=[
            pltpu.VMEM((blocks * LANES, width), jnp.bfloat16),
            pltpu.SemaphoreType.DMA((FAR,)),
        ],
        compiler_params=pltpu.CompilerParams(vmem_limit_bytes=50 * 2**20),
        cost_estimate=pl.CostEstimate(
            flops=4 * half * width * blocks * LANES,
            bytes_accessed=2 * width * (2 * half + FAR * columns) + 8 * half * blocks * LANES,
            transcendentals=0,
        ),
        name="far_sums",
    )(y_index.reshape(1), rows, weights)


def shift_y(step):
    return [
        (SIDE * x + y, SIDE * x + (y + step) % SIDE) for x in range(SIDE) for y in range(SIDE)
    ]


def local(tokens, q_weight, kv_weight, key_cache, value_cache, lengths):
    my_count = lax.axis_size("my")
    planes = my_count // 2
    own_rows = tokens.shape[0] // my_count
    width = tokens.shape[1]
    columns = q_weight.shape[1]
    head_size = key_cache.shape[2]
    slot_count = key_cache.shape[1]
    x_index = lax.axis_index("mx") // SIDE
    y_index = lax.axis_index("mx") % SIDE
    core = lax.axis_index("my") % 2

    x_rings = [[SIDE * x + y for x in range(SIDE)] for y in range(SIDE)]
    y_rings = [[SIDE * x + y for y in range(SIDE)] for x in range(SIDE)]
    core_pairs = [(i, i ^ 1) for i in range(my_count)]
    plane_groups = [
        [(SIDE * x + y) * my_count + 2 * plane + one for plane in range(planes) for x in range(SIDE)]
        for y in range(SIDE)
        for one in range(2)
    ]

    weights_here = lax.all_gather(q_weight, "mx", axis=1, tiled=True, axis_index_groups=y_rings)
    below = lax.ppermute(q_weight, "mx", shift_y(1))
    above = lax.ppermute(q_weight, "mx", shift_y(-1))
    halves = tokens.reshape(planes, 2, own_rows, width).transpose(1, 0, 2, 3)
    halves = jnp.where(core == 0, halves[::-1], halves)
    halves = halves.reshape(-1, width)
    gathered = lax.all_gather(halves, "mx", axis=0, tiled=True, axis_index_groups=x_rings)
    pair_columns = kv_weight.shape[1] // SIDE
    pair_weight = lax.dynamic_slice_in_dim(kv_weight, x_index * pair_columns, pair_columns, 1)

    rows = gathered.reshape(SIDE, 2, planes, own_rows, width).transpose(1, 2, 0, 3, 4)
    rows = rows.reshape(-1, width)

    def exchange(other_sums, same_sums):
        swapped = lax.ppermute(other_sums, "my", core_pairs)
        chip_sums = (same_sums + swapped).reshape(planes * SIDE, -1, other_sums.shape[1])
        parts = lax.all_to_all(
            chip_sums, ("mx", "my"), split_axis=0, concat_axis=0, axis_index_groups=plane_groups
        )
        sums = jnp.sum(parts.reshape(planes, SIDE, *parts.shape[1:]), axis=0)
        return sums.astype(jnp.bfloat16).reshape(SIDE, own_rows, -1)

    near = exchange(*near_sums(rows, below.T, q_weight.T, above.T, pair_weight.T))
    new_pairs = near[:, :, NEAR * columns :].transpose(1, 0, 2).reshape(own_rows, -1)
    near = near[:, :, : NEAR * columns].transpose(1, 0, 2)
    rows, near, new_pairs = lax.optimization_barrier((rows, near, new_pairs))
    far = exchange(*far_sums(y_index, rows, weights_here.T))
    far = far[:, :, : FAR * columns].transpose(1, 0, 2)
    query_rows = jnp.concatenate([near, far], axis=2).reshape(own_rows, SIDE, SIDE, columns)
    query_rows = jnp.concatenate([query_rows, query_rows], axis=2)
    query_rows = lax.dynamic_slice_in_dim(query_rows, (SIDE + 1 - y_index) % SIDE, SIDE, 2)
    queries = query_rows.reshape(own_rows, -1, head_size)

    new_key = new_pairs[:, :head_size]
    new_value = new_pairs[:, head_size:]
    scale_factor = 1.0 / math.sqrt(head_size)
    scores = (
        jnp.einsum("rhd,rcd->rhc", queries, key_cache, preferred_element_type=jnp.float32)
        * scale_factor
    )
    own_score = (
        jnp.einsum("rhd,rd->rh", queries, new_key, preferred_element_type=jnp.float32)
        * scale_factor
    )
    slot_index = lax.broadcasted_iota(jnp.int32, (1, 1, slot_count), 2)
    live_mask = slot_index < lengths[:, None, None]
    peak_score = jnp.maximum(jnp.max(jnp.where(live_mask, scores, -jnp.inf), axis=2), own_score)
    raw_weights = jnp.where(live_mask, jnp.exp(scores - peak_score[:, :, None]), 0.0)
    own_raw = jnp.exp(own_score - peak_score)
    totals = jnp.sum(raw_weights, axis=2) + own_raw
    weights = (raw_weights / totals[:, :, None]).astype(jnp.bfloat16)
    own_weight = (own_raw / totals).astype(jnp.bfloat16)
    blended = jnp.einsum("rhc,rcd->rhd", weights, value_cache, preferred_element_type=jnp.float32)
    blended = (
        blended
        + own_weight.astype(jnp.float32)[:, :, None] * new_value.astype(jnp.float32)[:, None, :]
    )
    return blended.astype(jnp.bfloat16).reshape(own_rows, -1)


def solution(mesh):
    return jax.shard_map(
        local,
        mesh=mesh,
        in_specs=(
            P("mx", "my"),
            P("my", "mx"),
            P("my", None),
            P(("mx", "my"), None, None),
            P(("mx", "my"), None, None),
            P(("mx", "my")),
        ),
        out_specs=P(("mx", "my"), None),
        check_vma=False,
    )
```

```python
import functools
import math

import jax
import jax.numpy as jnp
from jax import lax
from jax.experimental import pallas as pl
from jax.experimental.pallas import tpu as pltpu
from jax.sharding import PartitionSpec as P

SIDE = 8
LANES = 128
NEAR = 3
FAR = SIDE - NEAR


def times(rows, weights):
    return lax.dot_general(
        rows, weights, (((1,), (1,)), ((), ())), preferred_element_type=jnp.float32
    )


def near_body(
    planes, own_rows, core_ref, gathered_ref, below_ref, own_ref, above_ref, pair_ref,
    rows_ref, other_ref, same_ref, held,
):
    at = 0
    for piece in (below_ref, own_ref, above_ref, pair_ref):
        held[at : at + piece.shape[0], :] = piece[...]
        at += piece.shape[0]
    count = gathered_ref.shape[0]
    half = count // 2
    row_bits, x_bits = own_rows.bit_length() - 1, SIDE.bit_length() - 1
    plane_bits = planes.bit_length() - 1
    into = lax.broadcasted_iota(jnp.int32, (count, 1), 0)
    row = into & (own_rows - 1)
    x = (into >> row_bits) & (SIDE - 1)
    plane = (into >> (row_bits + x_bits)) & (planes - 1)
    same = into >> (row_bits + x_bits + plane_bits)
    core = jnp.where(same == 1, core_ref[0], 1 - core_ref[0])
    source = (((((x << plane_bits) + plane) << 1) + core) << row_bits) + row
    pick = lax.broadcasted_iota(jnp.int32, (count, count), 1) == source
    pick = jnp.where(pick, 1.0, 0.0).astype(jnp.bfloat16)
    rows = jnp.dot(pick, gathered_ref[...], preferred_element_type=jnp.float32)
    rows = rows.astype(jnp.bfloat16)
    rows_ref[...] = rows
    sums = times(rows, held[...])
    other_ref[...] = sums[:half]
    same_ref[...] = sums[half:]


def near_sums(planes, own_rows, core, gathered, *pieces):
    count, width = gathered.shape
    columns = sum(piece.shape[0] for piece in pieces)
    product = jax.ShapeDtypeStruct((count // 2, columns), jnp.float32)
    in_vmem = pl.BlockSpec(memory_space=pltpu.VMEM)
    return pl.pallas_call(
        functools.partial(near_body, planes, own_rows),
        in_specs=[pl.BlockSpec(memory_space=pltpu.SMEM)] + [in_vmem] * (1 + len(pieces)),
        out_specs=[in_vmem] * 3,
        out_shape=[jax.ShapeDtypeStruct(gathered.shape, gathered.dtype), product, product],
        scratch_shapes=[pltpu.VMEM((columns, width), jnp.bfloat16)],
        compiler_params=pltpu.CompilerParams(vmem_limit_bytes=16 * 2**20),
        cost_estimate=pl.CostEstimate(
            flops=2 * count * width * (columns + count),
            bytes_accessed=2 * width * (2 * count + columns) + 4 * count * columns,
            transcendentals=0,
        ),
        name="near_sums",
    )(core.reshape(1), gathered, *pieces)


def far_body(blocks, y_ref, rows_ref, weights_ref, other_ref, same_ref, held, sems):
    columns = weights_ref.shape[0] // SIDE
    half = rows_ref.shape[0] // 2
    copies = []
    for at in range(FAR):
        source = lax.rem(y_ref[0] + 2 + at, SIDE) * columns
        copies.append(
            pltpu.make_async_copy(
                weights_ref.at[pl.ds(pl.multiple_of(source, columns), columns), :],
                held.at[pl.ds(at * columns, columns), :],
                sems.at[at],
            )
        )
        copies[-1].start()
    rest = held.shape[0] - FAR * columns
    held[FAR * columns :, :] = jnp.zeros((rest, held.shape[1]), held.dtype)
    waited, done = 0, 0
    while done < blocks:
        last = min(done + 3, blocks)
        while waited < FAR and waited * columns < last * LANES:
            copies[waited].wait()
            waited += 1
        sums = times(rows_ref[...], held[done * LANES : last * LANES, :])
        for block in range(done, last):
            lanes = slice((block - done) * LANES, (block - done + 1) * LANES)
            place = pl.ds(block, half, stride=blocks)
            other_ref[place, :] = sums[:half, lanes]
            same_ref[place, :] = sums[half:, lanes]
        done = last


def far_sums(y_index, rows, weights):
    half, width = rows.shape[0] // 2, rows.shape[1]
    columns = weights.shape[0] // SIDE
    blocks = -(-FAR * columns // LANES)
    product = jax.ShapeDtypeStruct((half * blocks, LANES), jnp.float32)
    in_vmem = pl.BlockSpec(memory_space=pltpu.VMEM)
    return pl.pallas_call(
        functools.partial(far_body, blocks),
        in_specs=[
            pl.BlockSpec(memory_space=pltpu.SMEM),
            in_vmem,
            pl.BlockSpec(memory_space=pltpu.HBM),
        ],
        out_specs=[in_vmem, in_vmem],
        out_shape=[product, product],
        scratch_shapes=[
            pltpu.VMEM((blocks * LANES, width), jnp.bfloat16),
            pltpu.SemaphoreType.DMA((FAR,)),
        ],
        compiler_params=pltpu.CompilerParams(vmem_limit_bytes=50 * 2**20),
        cost_estimate=pl.CostEstimate(
            flops=4 * half * width * blocks * LANES,
            bytes_accessed=2 * width * (2 * half + FAR * columns) + 8 * half * blocks * LANES,
            transcendentals=0,
        ),
        name="far_sums",
    )(y_index.reshape(1), rows, weights)


def shift_y(step):
    return [
        (SIDE * x + y, SIDE * x + (y + step) % SIDE) for x in range(SIDE) for y in range(SIDE)
    ]


def local(tokens, q_weight, kv_weight, key_cache, value_cache, lengths):
    my_count = lax.axis_size("my")
    planes = my_count // 2
    own_rows = tokens.shape[0] // my_count
    width = tokens.shape[1]
    columns = q_weight.shape[1]
    head_size = key_cache.shape[2]
    slot_count = key_cache.shape[1]
    x_index = lax.axis_index("mx") // SIDE
    y_index = lax.axis_index("mx") % SIDE
    core = lax.axis_index("my") % 2

    x_rings = [[SIDE * x + y for x in range(SIDE)] for y in range(SIDE)]
    y_rings = [[SIDE * x + y for y in range(SIDE)] for x in range(SIDE)]
    core_pairs = [(i, i ^ 1) for i in range(my_count)]
    plane_groups = [
        [(SIDE * x + y) * my_count + 2 * plane + one for plane in range(planes) for x in range(SIDE)]
        for y in range(SIDE)
        for one in range(2)
    ]

    weights_here = lax.all_gather(q_weight, "mx", axis=1, tiled=True, axis_index_groups=y_rings)
    below = lax.ppermute(q_weight, "mx", shift_y(1))
    above = lax.ppermute(q_weight, "mx", shift_y(-1))
    gathered = lax.all_gather(tokens, "mx", axis=0, tiled=True, axis_index_groups=x_rings)
    pair_columns = kv_weight.shape[1] // SIDE
    pair_weight = lax.dynamic_slice_in_dim(kv_weight, x_index * pair_columns, pair_columns, 1)

    def chip_sums(other_sums, same_sums):
        swapped = lax.ppermute(other_sums, "my", core_pairs)
        return (same_sums + swapped).reshape(planes * SIDE, -1, other_sums.shape[1])

    def exchange(sums):
        parts = lax.all_to_all(
            sums, ("mx", "my"), split_axis=0, concat_axis=0, axis_index_groups=plane_groups
        )
        sums = jnp.sum(parts.reshape(planes, SIDE, *parts.shape[1:]), axis=0)
        return sums.astype(jnp.bfloat16).reshape(SIDE, own_rows, -1)

    rows, *near = near_sums(
        planes, own_rows, core, gathered, below.T, q_weight.T, above.T, pair_weight.T
    )
    near = exchange(chip_sums(*near))
    new_pairs = near[:, :, NEAR * columns :].transpose(1, 0, 2).reshape(own_rows, -1)
    near = near[:, :, : NEAR * columns].transpose(1, 0, 2)
    far = chip_sums(*far_sums(y_index, rows, weights_here.T))
    far, near, new_pairs = lax.optimization_barrier((far, near, new_pairs))
    far = exchange(far)
    far = far[:, :, : FAR * columns].transpose(1, 0, 2)
    query_rows = jnp.concatenate([near, far], axis=2).reshape(own_rows, SIDE, SIDE, columns)
    query_rows = jnp.concatenate([query_rows, query_rows], axis=2)
    query_rows = lax.dynamic_slice_in_dim(query_rows, (SIDE + 1 - y_index) % SIDE, SIDE, 2)
    queries = query_rows.reshape(own_rows, -1, head_size)

    new_key = new_pairs[:, :head_size]
    new_value = new_pairs[:, head_size:]
    scale_factor = 1.0 / math.sqrt(head_size)
    scores = (
        jnp.einsum("rhd,rcd->rhc", queries, key_cache, preferred_element_type=jnp.float32)
        * scale_factor
    )
    own_score = (
        jnp.einsum("rhd,rd->rh", queries, new_key, preferred_element_type=jnp.float32)
        * scale_factor
    )
    slot_index = lax.broadcasted_iota(jnp.int32, (1, 1, slot_count), 2)
    live_mask = slot_index < lengths[:, None, None]
    peak_score = jnp.maximum(jnp.max(jnp.where(live_mask, scores, -jnp.inf), axis=2), own_score)
    raw_weights = jnp.where(live_mask, jnp.exp(scores - peak_score[:, :, None]), 0.0)
    own_raw = jnp.exp(own_score - peak_score)
    totals = jnp.sum(raw_weights, axis=2) + own_raw
    weights = (raw_weights / totals[:, :, None]).astype(jnp.bfloat16)
    own_weight = (own_raw / totals).astype(jnp.bfloat16)
    blended = jnp.einsum("rhc,rcd->rhd", weights, value_cache, preferred_element_type=jnp.float32)
    blended = (
        blended
        + own_weight.astype(jnp.float32)[:, :, None] * new_value.astype(jnp.float32)[:, None, :]
    )
    return blended.astype(jnp.bfloat16).reshape(own_rows, -1)


def solution(mesh):
    return jax.shard_map(
        local,
        mesh=mesh,
        in_specs=(
            P("mx", "my"),
            P("my", "mx"),
            P("my", None),
            P(("mx", "my"), None, None),
            P(("mx", "my"), None, None),
            P(("mx", "my")),
        ),
        out_specs=P(("mx", "my"), None),
        check_vma=False,
    )
```

```python
import functools
import math

import jax
import jax.numpy as jnp
from jax import lax
from jax.experimental import pallas as pl
from jax.experimental.pallas import tpu as pltpu
from jax.sharding import PartitionSpec as P

SIDE = 8
LANES = 128
NEAR = 3
FAR = SIDE - NEAR


def times(rows, weights):
    return lax.dot_general(
        rows, weights, (((1,), (1,)), ((), ())), preferred_element_type=jnp.float32
    )


def near_body(
    planes, own_rows, core_ref, gathered_ref, below_ref, own_ref, above_ref, pair_ref,
    rows_ref, other_ref, same_ref, held,
):
    at = 0
    for piece in (below_ref, own_ref, above_ref, pair_ref):
        held[at : at + piece.shape[0], :] = piece[...]
        at += piece.shape[0]
    count = gathered_ref.shape[0]
    half = count // 2
    row_bits, x_bits = own_rows.bit_length() - 1, SIDE.bit_length() - 1
    plane_bits = planes.bit_length() - 1
    into = lax.broadcasted_iota(jnp.int32, (count, 1), 0)
    row = into & (own_rows - 1)
    x = (into >> row_bits) & (SIDE - 1)
    plane = (into >> (row_bits + x_bits)) & (planes - 1)
    same = into >> (row_bits + x_bits + plane_bits)
    core = jnp.where(same == 1, core_ref[0], 1 - core_ref[0])
    source = (((((x << plane_bits) + plane) << 1) + core) << row_bits) + row
    pick = lax.broadcasted_iota(jnp.int32, (count, count), 1) == source
    pick = jnp.where(pick, 1.0, 0.0).astype(jnp.bfloat16)
    rows = jnp.dot(pick, gathered_ref[...], preferred_element_type=jnp.float32)
    rows = rows.astype(jnp.bfloat16)
    rows_ref[...] = rows
    sums = times(rows, held[...])
    other_ref[...] = sums[:half]
    same_ref[...] = sums[half:]


def near_sums(planes, own_rows, core, gathered, *pieces):
    count, width = gathered.shape
    columns = sum(piece.shape[0] for piece in pieces)
    product = jax.ShapeDtypeStruct((count // 2, columns), jnp.float32)
    in_vmem = pl.BlockSpec(memory_space=pltpu.VMEM)
    return pl.pallas_call(
        functools.partial(near_body, planes, own_rows),
        in_specs=[pl.BlockSpec(memory_space=pltpu.SMEM)] + [in_vmem] * (1 + len(pieces)),
        out_specs=[in_vmem] * 3,
        out_shape=[jax.ShapeDtypeStruct(gathered.shape, gathered.dtype), product, product],
        scratch_shapes=[pltpu.VMEM((columns, width), jnp.bfloat16)],
        compiler_params=pltpu.CompilerParams(vmem_limit_bytes=16 * 2**20),
        cost_estimate=pl.CostEstimate(
            flops=2 * count * width * (columns + count),
            bytes_accessed=2 * width * (2 * count + columns) + 4 * count * columns,
            transcendentals=0,
        ),
        name="near_sums",
    )(core.reshape(1), gathered, *pieces)


def far_body(blocks, y_ref, rows_ref, weights_ref, other_ref, same_ref, held, sems):
    columns = weights_ref.shape[0] // SIDE
    half = rows_ref.shape[0] // 2
    copies = []
    for at in range(FAR):
        source = lax.rem(y_ref[0] + 2 + at, SIDE) * columns
        copies.append(
            pltpu.make_async_copy(
                weights_ref.at[pl.ds(pl.multiple_of(source, columns), columns), :],
                held.at[pl.ds(at * columns, columns), :],
                sems.at[at],
            )
        )
        copies[-1].start()
    rest = held.shape[0] - FAR * columns
    held[FAR * columns :, :] = jnp.zeros((rest, held.shape[1]), held.dtype)
    for copy in copies:
        copy.wait()
    sums = times(rows_ref[...], held[...])
    for block in range(blocks):
        lanes = slice(block * LANES, (block + 1) * LANES)
        place = pl.ds(block, half, stride=blocks)
        other_ref[place, :] = sums[:half, lanes]
        same_ref[place, :] = sums[half:, lanes]


def far_sums(y_index, rows, weights):
    half, width = rows.shape[0] // 2, rows.shape[1]
    columns = weights.shape[0] // SIDE
    blocks = -(-FAR * columns // LANES)
    product = jax.ShapeDtypeStruct((half * blocks, LANES), jnp.float32)
    in_vmem = pl.BlockSpec(memory_space=pltpu.VMEM)
    return pl.pallas_call(
        functools.partial(far_body, blocks),
        in_specs=[
            pl.BlockSpec(memory_space=pltpu.SMEM),
            in_vmem,
            pl.BlockSpec(memory_space=pltpu.HBM),
        ],
        out_specs=[in_vmem, in_vmem],
        out_shape=[product, product],
        scratch_shapes=[
            pltpu.VMEM((blocks * LANES, width), jnp.bfloat16),
            pltpu.SemaphoreType.DMA((FAR,)),
        ],
        compiler_params=pltpu.CompilerParams(vmem_limit_bytes=50 * 2**20),
        cost_estimate=pl.CostEstimate(
            flops=4 * half * width * blocks * LANES,
            bytes_accessed=2 * width * (2 * half + FAR * columns) + 8 * half * blocks * LANES,
            transcendentals=0,
        ),
        name="far_sums",
    )(y_index.reshape(1), rows, weights)


def attend_body(lengths_ref, queries_ref, pairs_ref, keys_ref, values_ref, out_ref):
    own_rows, _, head_size = queries_ref.shape
    scale_factor = 1.0 / math.sqrt(head_size)
    shares = []
    for row in range(own_rows):
        queries = queries_ref[row]
        scores = times(queries, keys_ref[row]) * scale_factor
        new_key = pairs_ref[row : row + 1, :head_size].astype(jnp.float32)
        own_score = jnp.sum(queries.astype(jnp.float32) * new_key, axis=1, keepdims=True)
        own_score = own_score * scale_factor
        live_mask = lax.broadcasted_iota(jnp.int32, scores.shape, 1) < lengths_ref[row]
        peak_score = jnp.max(jnp.where(live_mask, scores, -jnp.inf), axis=1, keepdims=True)
        peak_score = jnp.maximum(peak_score, own_score)
        raw_weights = jnp.where(live_mask, jnp.exp(scores - peak_score), 0.0)
        own_raw = jnp.exp(own_score - peak_score)
        totals = jnp.sum(raw_weights, axis=1, keepdims=True) + own_raw
        weights = (raw_weights / totals).astype(jnp.bfloat16)
        shares.append((weights, (own_raw / totals).astype(jnp.bfloat16)))
    for row, (weights, own_weight) in enumerate(shares):
        new_value = pairs_ref[row : row + 1, head_size:].astype(jnp.float32)
        blended = jnp.dot(weights, values_ref[row], preferred_element_type=jnp.float32)
        blended = blended + own_weight.astype(jnp.float32) * new_value
        out_ref[row] = blended.astype(out_ref.dtype)


def attend(lengths, queries, new_pairs, key_cache, value_cache):
    in_vmem = pl.BlockSpec(memory_space=pltpu.VMEM)
    return pl.pallas_call(
        attend_body,
        in_specs=[pl.BlockSpec(memory_space=pltpu.SMEM)] + [in_vmem] * 4,
        out_specs=in_vmem,
        out_shape=jax.ShapeDtypeStruct(queries.shape, queries.dtype),
        compiler_params=pltpu.CompilerParams(vmem_limit_bytes=8 * 2**20),
        cost_estimate=pl.CostEstimate(
            flops=4 * queries.shape[1] * key_cache.size,
            bytes_accessed=4 * key_cache.size,
            transcendentals=queries.shape[0] * queries.shape[1] * key_cache.shape[1],
        ),
        name="attend",
    )(lengths, queries, new_pairs, key_cache, value_cache)


def shift_y(step):
    return [
        (SIDE * x + y, SIDE * x + (y + step) % SIDE) for x in range(SIDE) for y in range(SIDE)
    ]


def local(tokens, q_weight, kv_weight, key_cache, value_cache, lengths):
    my_count = lax.axis_size("my")
    planes = my_count // 2
    own_rows = tokens.shape[0] // my_count
    width = tokens.shape[1]
    columns = q_weight.shape[1]
    head_size = key_cache.shape[2]
    x_index = lax.axis_index("mx") // SIDE
    y_index = lax.axis_index("mx") % SIDE
    core = lax.axis_index("my") % 2

    x_rings = [[SIDE * x + y for x in range(SIDE)] for y in range(SIDE)]
    y_rings = [[SIDE * x + y for y in range(SIDE)] for x in range(SIDE)]
    core_pairs = [(i, i ^ 1) for i in range(my_count)]
    plane_groups = [
        [(SIDE * x + y) * my_count + 2 * plane + one for plane in range(planes) for x in range(SIDE)]
        for y in range(SIDE)
        for one in range(2)
    ]

    weights_here = lax.all_gather(q_weight, "mx", axis=1, tiled=True, axis_index_groups=y_rings)
    below = lax.ppermute(q_weight, "mx", shift_y(1))
    above = lax.ppermute(q_weight, "mx", shift_y(-1))
    gathered = lax.all_gather(tokens, "mx", axis=0, tiled=True, axis_index_groups=x_rings)
    pair_columns = kv_weight.shape[1] // SIDE
    pair_weight = lax.dynamic_slice_in_dim(kv_weight, x_index * pair_columns, pair_columns, 1)

    def chip_sums(other_sums, same_sums):
        swapped = lax.ppermute(other_sums, "my", core_pairs)
        return (same_sums + swapped).reshape(planes * SIDE, -1, other_sums.shape[1])

    def exchange(sums):
        parts = lax.all_to_all(
            sums, ("mx", "my"), split_axis=0, concat_axis=0, axis_index_groups=plane_groups
        )
        sums = jnp.sum(parts.reshape(planes, SIDE, *parts.shape[1:]), axis=0)
        return sums.astype(jnp.bfloat16).reshape(SIDE, own_rows, -1)

    rows, *near = near_sums(
        planes, own_rows, core, gathered, below.T, q_weight.T, above.T, pair_weight.T
    )
    near = exchange(chip_sums(*near))
    new_pairs = near[:, :, NEAR * columns :].transpose(1, 0, 2).reshape(own_rows, -1)
    near = near[:, :, : NEAR * columns].transpose(1, 0, 2)
    far = chip_sums(*far_sums(y_index, rows, weights_here.T))
    far, near, new_pairs = lax.optimization_barrier((far, near, new_pairs))
    far = exchange(far)
    far = far[:, :, : FAR * columns].transpose(1, 0, 2)
    query_rows = jnp.concatenate([near, far], axis=2).reshape(own_rows, SIDE, SIDE, columns)
    query_rows = jnp.concatenate([query_rows, query_rows], axis=2)
    query_rows = lax.dynamic_slice_in_dim(query_rows, (SIDE + 1 - y_index) % SIDE, SIDE, 2)
    queries = query_rows.reshape(own_rows, -1, head_size)

    return attend(lengths, queries, new_pairs, key_cache, value_cache).reshape(own_rows, -1)


def solution(mesh):
    return jax.shard_map(
        local,
        mesh=mesh,
        in_specs=(
            P("mx", "my"),
            P("my", "mx"),
            P("my", None),
            P(("mx", "my"), None, None),
            P(("mx", "my"), None, None),
            P(("mx", "my")),
        ),
        out_specs=P(("mx", "my"), None),
        check_vma=False,
    )
```

```python
import functools
import math

import jax
import jax.numpy as jnp
from jax import lax
from jax.experimental import pallas as pl
from jax.experimental.pallas import tpu as pltpu
from jax.sharding import PartitionSpec as P

SIDE = 8
LANES = 128
NEAR = 3
FAR = SIDE - NEAR


def times(rows, weights):
    return lax.dot_general(
        rows, weights, (((1,), (1,)), ((), ())), preferred_element_type=jnp.float32
    )


def near_body(
    planes, own_rows, core_ref, gathered_ref, below_ref, own_ref, above_ref, pair_ref,
    rows_ref, other_ref, same_ref, held,
):
    at = 0
    for piece in (below_ref, own_ref, above_ref, pair_ref):
        held[at : at + piece.shape[0], :] = piece[...]
        at += piece.shape[0]
    count = gathered_ref.shape[0]
    half = count // 2
    row_bits, x_bits = own_rows.bit_length() - 1, SIDE.bit_length() - 1
    plane_bits = planes.bit_length() - 1
    into = lax.broadcasted_iota(jnp.int32, (count, 1), 0)
    row = into & (own_rows - 1)
    x = (into >> row_bits) & (SIDE - 1)
    plane = (into >> (row_bits + x_bits)) & (planes - 1)
    same = into >> (row_bits + x_bits + plane_bits)
    core = jnp.where(same == 1, core_ref[0], 1 - core_ref[0])
    source = (((((x << plane_bits) + plane) << 1) + core) << row_bits) + row
    pick = lax.broadcasted_iota(jnp.int32, (count, count), 1) == source
    pick = jnp.where(pick, 1.0, 0.0).astype(jnp.bfloat16)
    rows = jnp.dot(pick, gathered_ref[...], preferred_element_type=jnp.float32)
    rows = rows.astype(jnp.bfloat16)
    rows_ref[...] = rows
    sums = times(rows, held[...])
    other_ref[...] = sums[:half]
    same_ref[...] = sums[half:]


def near_sums(planes, own_rows, core, gathered, *pieces):
    count, width = gathered.shape
    columns = sum(piece.shape[0] for piece in pieces)
    product = jax.ShapeDtypeStruct((count // 2, columns), jnp.float32)
    in_vmem = pl.BlockSpec(memory_space=pltpu.VMEM)
    return pl.pallas_call(
        functools.partial(near_body, planes, own_rows),
        in_specs=[pl.BlockSpec(memory_space=pltpu.SMEM)] + [in_vmem] * (1 + len(pieces)),
        out_specs=[in_vmem] * 3,
        out_shape=[jax.ShapeDtypeStruct(gathered.shape, gathered.dtype), product, product],
        scratch_shapes=[pltpu.VMEM((columns, width), jnp.bfloat16)],
        compiler_params=pltpu.CompilerParams(vmem_limit_bytes=16 * 2**20),
        cost_estimate=pl.CostEstimate(
            flops=2 * count * width * (columns + count),
            bytes_accessed=2 * width * (2 * count + columns) + 4 * count * columns,
            transcendentals=0,
        ),
        name="near_sums",
    )(core.reshape(1), gathered, *pieces)


def far_body(blocks, rows_ref, *refs):
    *pieces, other_ref, same_ref, held = refs
    half = rows_ref.shape[0] // 2
    at = 0
    for piece in pieces:
        held[at : at + piece.shape[0], :] = piece[...]
        at += piece.shape[0]
    held[at:, :] = jnp.zeros((held.shape[0] - at, held.shape[1]), held.dtype)
    sums = times(rows_ref[...], held[...])
    for block in range(blocks):
        lanes = slice(block * LANES, (block + 1) * LANES)
        place = pl.ds(block, half, stride=blocks)
        other_ref[place, :] = sums[:half, lanes]
        same_ref[place, :] = sums[half:, lanes]


def far_sums(rows, *pieces):
    half, width = rows.shape[0] // 2, rows.shape[1]
    blocks = -(-sum(piece.shape[0] for piece in pieces) // LANES)
    product = jax.ShapeDtypeStruct((half * blocks, LANES), jnp.float32)
    in_vmem = pl.BlockSpec(memory_space=pltpu.VMEM)
    return pl.pallas_call(
        functools.partial(far_body, blocks),
        in_specs=[in_vmem] * (1 + len(pieces)),
        out_specs=[in_vmem, in_vmem],
        out_shape=[product, product],
        scratch_shapes=[pltpu.VMEM((blocks * LANES, width), jnp.bfloat16)],
        compiler_params=pltpu.CompilerParams(vmem_limit_bytes=20 * 2**20),
        cost_estimate=pl.CostEstimate(
            flops=4 * half * width * blocks * LANES,
            bytes_accessed=2 * width * (2 * half + blocks * LANES) + 8 * half * blocks * LANES,
            transcendentals=0,
        ),
        name="far_sums",
    )(rows, *pieces)


def attend_body(lengths_ref, queries_ref, pairs_ref, keys_ref, values_ref, out_ref):
    own_rows, _, head_size = queries_ref.shape
    scale_factor = 1.0 / math.sqrt(head_size)
    shares = []
    for row in range(own_rows):
        queries = queries_ref[row]
        scores = times(queries, keys_ref[row]) * scale_factor
        new_key = pairs_ref[row : row + 1, :head_size].astype(jnp.float32)
        own_score = jnp.sum(queries.astype(jnp.float32) * new_key, axis=1, keepdims=True)
        own_score = own_score * scale_factor
        live_mask = lax.broadcasted_iota(jnp.int32, scores.shape, 1) < lengths_ref[row]
        peak_score = jnp.max(jnp.where(live_mask, scores, -jnp.inf), axis=1, keepdims=True)
        peak_score = jnp.maximum(peak_score, own_score)
        raw_weights = jnp.where(live_mask, jnp.exp(scores - peak_score), 0.0)
        own_raw = jnp.exp(own_score - peak_score)
        totals = jnp.sum(raw_weights, axis=1, keepdims=True) + own_raw
        weights = (raw_weights / totals).astype(jnp.bfloat16)
        shares.append((weights, (own_raw / totals).astype(jnp.bfloat16)))
    for row, (weights, own_weight) in enumerate(shares):
        new_value = pairs_ref[row : row + 1, head_size:].astype(jnp.float32)
        blended = jnp.dot(weights, values_ref[row], preferred_element_type=jnp.float32)
        blended = blended + own_weight.astype(jnp.float32) * new_value
        out_ref[row] = blended.astype(out_ref.dtype)


def attend(lengths, queries, new_pairs, key_cache, value_cache):
    in_vmem = pl.BlockSpec(memory_space=pltpu.VMEM)
    return pl.pallas_call(
        attend_body,
        in_specs=[pl.BlockSpec(memory_space=pltpu.SMEM)] + [in_vmem] * 4,
        out_specs=in_vmem,
        out_shape=jax.ShapeDtypeStruct(queries.shape, queries.dtype),
        compiler_params=pltpu.CompilerParams(vmem_limit_bytes=8 * 2**20),
        cost_estimate=pl.CostEstimate(
            flops=4 * queries.shape[1] * key_cache.size,
            bytes_accessed=4 * key_cache.size,
            transcendentals=queries.shape[0] * queries.shape[1] * key_cache.shape[1],
        ),
        name="attend",
    )(lengths, queries, new_pairs, key_cache, value_cache)


def shift_y(step):
    return [
        (SIDE * x + y, SIDE * x + (y + step) % SIDE) for x in range(SIDE) for y in range(SIDE)
    ]


def local(tokens, q_weight, kv_weight, key_cache, value_cache, lengths):
    my_count = lax.axis_size("my")
    planes = my_count // 2
    own_rows = tokens.shape[0] // my_count
    width = tokens.shape[1]
    columns = q_weight.shape[1]
    head_size = key_cache.shape[2]
    x_index = lax.axis_index("mx") // SIDE
    y_index = lax.axis_index("mx") % SIDE
    core = lax.axis_index("my") % 2

    x_rings = [[SIDE * x + y for x in range(SIDE)] for y in range(SIDE)]
    core_pairs = [(i, i ^ 1) for i in range(my_count)]
    plane_groups = [
        [(SIDE * x + y) * my_count + 2 * plane + one for plane in range(planes) for x in range(SIDE)]
        for y in range(SIDE)
        for one in range(2)
    ]

    below = [lax.ppermute(q_weight, "mx", shift_y(1))]
    above = [lax.ppermute(q_weight, "mx", shift_y(-1))]
    copies = jnp.broadcast_to(tokens, (SIDE, *tokens.shape))
    gathered = lax.all_to_all(
        copies, "mx", split_axis=0, concat_axis=0, axis_index_groups=x_rings
    ).reshape(-1, width)
    for _ in range(2):
        below.append(lax.ppermute(below[-1], "mx", shift_y(1)))
        above.append(lax.ppermute(above[-1], "mx", shift_y(-1)))
    half = columns // 2
    opposite = (
        lax.ppermute(below[2][:, :half], "mx", shift_y(1)),
        lax.ppermute(above[2][:, half:], "mx", shift_y(-1)),
    )
    pair_columns = kv_weight.shape[1] // SIDE
    pair_weight = lax.dynamic_slice_in_dim(kv_weight, x_index * pair_columns, pair_columns, 1)

    def chip_sums(other_sums, same_sums):
        swapped = lax.ppermute(other_sums, "my", core_pairs)
        return (same_sums + swapped).reshape(planes * SIDE, -1, other_sums.shape[1])

    def exchange(sums):
        parts = lax.all_to_all(
            sums, ("mx", "my"), split_axis=0, concat_axis=0, axis_index_groups=plane_groups
        )
        sums = jnp.sum(parts.reshape(planes, SIDE, *parts.shape[1:]), axis=0)
        return sums.astype(jnp.bfloat16).reshape(SIDE, own_rows, -1)

    rows, *near = near_sums(
        planes, own_rows, core, gathered, below[0].T, q_weight.T, above[0].T, pair_weight.T
    )
    near = exchange(chip_sums(*near))
    new_pairs = near[:, :, NEAR * columns :].transpose(1, 0, 2).reshape(own_rows, -1)
    near = near[:, :, : NEAR * columns].transpose(1, 0, 2)
    pieces = above[1], above[2], *opposite, below[2], below[1]
    far = chip_sums(*far_sums(rows, *(piece.T for piece in pieces)))
    far, near, new_pairs = lax.optimization_barrier((far, near, new_pairs))
    far = exchange(far)
    far = far[:, :, : FAR * columns].transpose(1, 0, 2)
    query_rows = jnp.concatenate([near, far], axis=2).reshape(own_rows, SIDE, SIDE, columns)
    query_rows = jnp.concatenate([query_rows, query_rows], axis=2)
    query_rows = lax.dynamic_slice_in_dim(query_rows, (SIDE + 1 - y_index) % SIDE, SIDE, 2)
    queries = query_rows.reshape(own_rows, -1, head_size)

    return attend(lengths, queries, new_pairs, key_cache, value_cache).reshape(own_rows, -1)


def solution(mesh):
    return jax.shard_map(
        local,
        mesh=mesh,
        in_specs=(
            P("mx", "my"),
            P("my", "mx"),
            P("my", None),
            P(("mx", "my"), None, None),
            P(("mx", "my"), None, None),
            P(("mx", "my")),
        ),
        out_specs=P(("mx", "my"), None),
        check_vma=False,
    )
```

```python
import functools
import math

import jax
import jax.numpy as jnp
from jax import lax
from jax.experimental import pallas as pl
from jax.experimental.pallas import tpu as pltpu
from jax.sharding import PartitionSpec as P

SIDE = 8


LANES = 128


def times(rows, weights):
    return lax.dot_general(
        rows, weights, (((1,), (1,)), ((), ())), preferred_element_type=jnp.float32
    )


def strip_body(
    planes, own_rows, core_ref, gathered_ref, *refs,
):
    *pieces, other_ref, same_ref, held = refs
    at = 0
    for piece in pieces:
        held[at : at + piece.shape[0], :] = piece[...]
        at += piece.shape[0]
    held[at:, :] = jnp.zeros((held.shape[0] - at, held.shape[1]), held.dtype)
    count = gathered_ref.shape[0]
    half = count // 2
    row_bits, x_bits = own_rows.bit_length() - 1, SIDE.bit_length() - 1
    plane_bits = planes.bit_length() - 1
    into = lax.broadcasted_iota(jnp.int32, (count, 1), 0)
    row = into & (own_rows - 1)
    x = (into >> row_bits) & (SIDE - 1)
    plane = (into >> (row_bits + x_bits)) & (planes - 1)
    same = into >> (row_bits + x_bits + plane_bits)
    core = jnp.where(same == 1, core_ref[0], 1 - core_ref[0])
    source = (((((x << plane_bits) + plane) << 1) + core) << row_bits) + row
    pick = lax.broadcasted_iota(jnp.int32, (count, count), 1) == source
    pick = jnp.where(pick, 1.0, 0.0).astype(jnp.bfloat16)
    rows = jnp.dot(pick, gathered_ref[...], preferred_element_type=jnp.float32)
    rows = rows.astype(jnp.bfloat16)
    sums = times(rows, held[...])
    other_ref[...] = sums[:half]
    same_ref[...] = sums[half:]


def strip_sums(planes, own_rows, core, gathered, *pieces):
    count, width = gathered.shape
    columns = -(-sum(piece.shape[0] for piece in pieces) // LANES) * LANES
    product = jax.ShapeDtypeStruct((count // 2, columns), jnp.float32)
    in_vmem = pl.BlockSpec(memory_space=pltpu.VMEM)
    return pl.pallas_call(
        functools.partial(strip_body, planes, own_rows),
        in_specs=[pl.BlockSpec(memory_space=pltpu.SMEM)] + [in_vmem] * (1 + len(pieces)),
        out_specs=[in_vmem] * 2,
        out_shape=[product, product],
        scratch_shapes=[pltpu.VMEM((columns, width), jnp.bfloat16)],
        compiler_params=pltpu.CompilerParams(vmem_limit_bytes=24 * 2**20),
        cost_estimate=pl.CostEstimate(
            flops=2 * count * width * (columns + count),
            bytes_accessed=2 * width * (2 * count + columns) + 4 * count * columns,
            transcendentals=0,
        ),
        name="strip_sums",
    )(core.reshape(1), gathered, *pieces)


def attend_body(lengths_ref, queries_ref, pairs_ref, keys_ref, values_ref, out_ref):
    own_rows, _, head_size = queries_ref.shape
    scale_factor = 1.0 / math.sqrt(head_size)
    shares = []
    for row in range(own_rows):
        queries = queries_ref[row]
        scores = times(queries, keys_ref[row]) * scale_factor
        new_key = pairs_ref[row : row + 1, :head_size].astype(jnp.float32)
        own_score = jnp.sum(queries.astype(jnp.float32) * new_key, axis=1, keepdims=True)
        own_score = own_score * scale_factor
        live_mask = lax.broadcasted_iota(jnp.int32, scores.shape, 1) < lengths_ref[row]
        peak_score = jnp.max(jnp.where(live_mask, scores, -jnp.inf), axis=1, keepdims=True)
        peak_score = jnp.maximum(peak_score, own_score)
        raw_weights = jnp.where(live_mask, jnp.exp(scores - peak_score), 0.0)
        own_raw = jnp.exp(own_score - peak_score)
        totals = jnp.sum(raw_weights, axis=1, keepdims=True) + own_raw
        weights = (raw_weights / totals).astype(jnp.bfloat16)
        shares.append((weights, (own_raw / totals).astype(jnp.bfloat16)))
    for row, (weights, own_weight) in enumerate(shares):
        new_value = pairs_ref[row : row + 1, head_size:].astype(jnp.float32)
        blended = jnp.dot(weights, values_ref[row], preferred_element_type=jnp.float32)
        blended = blended + own_weight.astype(jnp.float32) * new_value
        out_ref[row] = blended.astype(out_ref.dtype)


def attend(lengths, queries, new_pairs, key_cache, value_cache):
    in_vmem = pl.BlockSpec(memory_space=pltpu.VMEM)
    return pl.pallas_call(
        attend_body,
        in_specs=[pl.BlockSpec(memory_space=pltpu.SMEM)] + [in_vmem] * 4,
        out_specs=in_vmem,
        out_shape=jax.ShapeDtypeStruct(queries.shape, queries.dtype),
        compiler_params=pltpu.CompilerParams(vmem_limit_bytes=8 * 2**20),
        cost_estimate=pl.CostEstimate(
            flops=4 * queries.shape[1] * key_cache.size,
            bytes_accessed=4 * key_cache.size,
            transcendentals=queries.shape[0] * queries.shape[1] * key_cache.shape[1],
        ),
        name="attend",
    )(lengths, queries, new_pairs, key_cache, value_cache)


def shift_y(step):
    return [
        (SIDE * x + y, SIDE * x + (y + step) % SIDE) for x in range(SIDE) for y in range(SIDE)
    ]


def local(tokens, q_weight, kv_weight, key_cache, value_cache, lengths):
    my_count = lax.axis_size("my")
    planes = my_count // 2
    own_rows = tokens.shape[0] // my_count
    width = tokens.shape[1]
    columns = q_weight.shape[1]
    head_size = key_cache.shape[2]
    x_index = lax.axis_index("mx") // SIDE
    y_index = lax.axis_index("mx") % SIDE
    core = lax.axis_index("my") % 2

    x_rings = [[SIDE * x + y for x in range(SIDE)] for y in range(SIDE)]
    core_pairs = [(i, i ^ 1) for i in range(my_count)]
    plane_groups = [
        [(SIDE * x + y) * my_count + 2 * plane + one for plane in range(planes) for x in range(SIDE)]
        for y in range(SIDE)
        for one in range(2)
    ]

    below = [lax.ppermute(q_weight, "mx", shift_y(1))]
    above = [lax.ppermute(q_weight, "mx", shift_y(-1))]
    tokens, below[0], above[0] = lax.optimization_barrier((tokens, below[0], above[0]))
    copies = jnp.broadcast_to(tokens, (SIDE, *tokens.shape))
    gathered = lax.all_to_all(
        copies, "mx", split_axis=0, concat_axis=0, axis_index_groups=x_rings
    ).reshape(-1, width)
    for _ in range(2):
        below.append(lax.ppermute(below[-1], "mx", shift_y(1)))
        above.append(lax.ppermute(above[-1], "mx", shift_y(-1)))
    half = columns // 2
    opposite = (
        lax.ppermute(below[2][:, :half], "mx", shift_y(1)),
        lax.ppermute(above[2][:, half:], "mx", shift_y(-1)),
    )
    pair_columns = kv_weight.shape[1] // SIDE
    pair_weight = lax.dynamic_slice_in_dim(kv_weight, x_index * pair_columns, pair_columns, 1)

    def chip_sums(other_sums, same_sums):
        swapped = lax.ppermute(other_sums, "my", core_pairs)
        return (same_sums + swapped).reshape(planes * SIDE, -1, other_sums.shape[1])

    def exchange(sums):
        parts = lax.all_to_all(
            sums, ("mx", "my"), split_axis=0, concat_axis=0, axis_index_groups=plane_groups
        )
        sums = jnp.sum(parts.reshape(planes, SIDE, *parts.shape[1:]), axis=0)
        return sums.astype(jnp.bfloat16).reshape(SIDE, own_rows, -1)

    pieces = (
        below[0], q_weight, above[0], above[1], above[2], *opposite, below[2], below[1], pair_weight
    )
    sums = strip_sums(planes, own_rows, core, gathered, *(piece.T for piece in pieces))
    strip = exchange(chip_sums(*sums))
    new_pairs = strip[:, :, SIDE * columns : SIDE * columns + pair_columns].transpose(1, 0, 2).reshape(own_rows, -1)
    query_rows = strip[:, :, : SIDE * columns].transpose(1, 0, 2)
    query_rows = query_rows.reshape(own_rows, SIDE, SIDE, columns)
    query_rows = jnp.concatenate([query_rows, query_rows], axis=2)
    query_rows = lax.dynamic_slice_in_dim(query_rows, (SIDE + 1 - y_index) % SIDE, SIDE, 2)
    queries = query_rows.reshape(own_rows, -1, head_size)

    return attend(lengths, queries, new_pairs, key_cache, value_cache).reshape(own_rows, -1)


def solution(mesh):
    return jax.shard_map(
        local,
        mesh=mesh,
        in_specs=(
            P("mx", "my"),
            P("my", "mx"),
            P("my", None),
            P(("mx", "my"), None, None),
            P(("mx", "my"), None, None),
            P(("mx", "my")),
        ),
        out_specs=P(("mx", "my"), None),
        check_vma=False,
    )
```

```python
import functools
import math

import jax
import jax.numpy as jnp
from jax import lax
from jax.experimental import pallas as pl
from jax.experimental.pallas import tpu as pltpu
from jax.sharding import PartitionSpec as P

SIDE = 8


LANES = 128


def times(rows, weights):
    return lax.dot_general(
        rows, weights, (((1,), (1,)), ((), ())), preferred_element_type=jnp.float32
    )


def strip_body(
    planes, own_rows, core_ref, gathered_ref, *refs,
):
    *pieces, other_ref, same_ref, held = refs
    at = 0
    for piece in pieces:
        held[at : at + piece.shape[0], :] = piece[...]
        at += piece.shape[0]
    if at < held.shape[0]:
        held[at:, :] = jnp.zeros((held.shape[0] - at, held.shape[1]), held.dtype)
    count = gathered_ref.shape[0]
    half = count // 2
    row_bits, x_bits = own_rows.bit_length() - 1, SIDE.bit_length() - 1
    plane_bits = planes.bit_length() - 1
    into = lax.broadcasted_iota(jnp.int32, (count, 1), 0)
    row = into & (own_rows - 1)
    x = (into >> row_bits) & (SIDE - 1)
    plane = (into >> (row_bits + x_bits)) & (planes - 1)
    same = into >> (row_bits + x_bits + plane_bits)
    core = jnp.where(same == 1, core_ref[0], 1 - core_ref[0])
    source = (((((x << plane_bits) + plane) << 1) + core) << row_bits) + row
    pick = lax.broadcasted_iota(jnp.int32, (count, count), 1) == source
    pick = jnp.where(pick, 1.0, 0.0).astype(jnp.bfloat16)
    rows = jnp.dot(pick, gathered_ref[...], preferred_element_type=jnp.float32)
    rows = rows.astype(jnp.bfloat16)
    sums = times(rows, held[...])
    other_ref[...] = sums[:half]
    same_ref[...] = sums[half:]


def strip_sums(planes, own_rows, core, gathered, *pieces):
    count, width = gathered.shape
    columns = -(-sum(piece.shape[0] for piece in pieces) // LANES) * LANES
    product = jax.ShapeDtypeStruct((count // 2, columns), jnp.float32)
    in_vmem = pl.BlockSpec(memory_space=pltpu.VMEM)
    return pl.pallas_call(
        functools.partial(strip_body, planes, own_rows),
        in_specs=[pl.BlockSpec(memory_space=pltpu.SMEM)] + [in_vmem] * (1 + len(pieces)),
        out_specs=[in_vmem] * 2,
        out_shape=[product, product],
        scratch_shapes=[pltpu.VMEM((columns, width), jnp.bfloat16)],
        compiler_params=pltpu.CompilerParams(vmem_limit_bytes=24 * 2**20),
        cost_estimate=pl.CostEstimate(
            flops=2 * count * width * (columns + count),
            bytes_accessed=2 * width * (2 * count + columns) + 4 * count * columns,
            transcendentals=0,
        ),
        name="strip_sums",
    )(core.reshape(1), gathered, *pieces)


def attend_body(lengths_ref, queries_ref, pairs_ref, keys_ref, values_ref, out_ref):
    own_rows, _, head_size = queries_ref.shape
    scale_factor = 1.0 / math.sqrt(head_size)
    shares = []
    for row in range(own_rows):
        queries = queries_ref[row]
        scores = times(queries, keys_ref[row]) * scale_factor
        new_key = pairs_ref[row : row + 1, :head_size].astype(jnp.float32)
        own_score = jnp.sum(queries.astype(jnp.float32) * new_key, axis=1, keepdims=True)
        own_score = own_score * scale_factor
        live_mask = lax.broadcasted_iota(jnp.int32, scores.shape, 1) < lengths_ref[row]
        peak_score = jnp.max(jnp.where(live_mask, scores, -jnp.inf), axis=1, keepdims=True)
        peak_score = jnp.maximum(peak_score, own_score)
        raw_weights = jnp.where(live_mask, jnp.exp(scores - peak_score), 0.0)
        own_raw = jnp.exp(own_score - peak_score)
        totals = jnp.sum(raw_weights, axis=1, keepdims=True) + own_raw
        weights = (raw_weights / totals).astype(jnp.bfloat16)
        shares.append((weights, (own_raw / totals).astype(jnp.bfloat16)))
    for row, (weights, own_weight) in enumerate(shares):
        new_value = pairs_ref[row : row + 1, head_size:].astype(jnp.float32)
        blended = jnp.dot(weights, values_ref[row], preferred_element_type=jnp.float32)
        blended = blended + own_weight.astype(jnp.float32) * new_value
        out_ref[row] = blended.astype(out_ref.dtype)


def attend(lengths, queries, new_pairs, key_cache, value_cache):
    in_vmem = pl.BlockSpec(memory_space=pltpu.VMEM)
    return pl.pallas_call(
        attend_body,
        in_specs=[pl.BlockSpec(memory_space=pltpu.SMEM)] + [in_vmem] * 4,
        out_specs=in_vmem,
        out_shape=jax.ShapeDtypeStruct(queries.shape, queries.dtype),
        compiler_params=pltpu.CompilerParams(vmem_limit_bytes=8 * 2**20),
        cost_estimate=pl.CostEstimate(
            flops=4 * queries.shape[1] * key_cache.size,
            bytes_accessed=4 * key_cache.size,
            transcendentals=queries.shape[0] * queries.shape[1] * key_cache.shape[1],
        ),
        name="attend",
    )(lengths, queries, new_pairs, key_cache, value_cache)


def shift_y(step):
    return [
        (SIDE * x + y, SIDE * x + (y + step) % SIDE) for x in range(SIDE) for y in range(SIDE)
    ]


def local(tokens, q_weight, kv_weight, key_cache, value_cache, lengths):
    my_count = lax.axis_size("my")
    planes = my_count // 2
    own_rows = tokens.shape[0] // my_count
    width = tokens.shape[1]
    columns = q_weight.shape[1]
    head_size = key_cache.shape[2]
    x_index = lax.axis_index("mx") // SIDE
    y_index = lax.axis_index("mx") % SIDE
    core = lax.axis_index("my") % 2

    x_rings = [[SIDE * x + y for x in range(SIDE)] for y in range(SIDE)]
    core_pairs = [(i, i ^ 1) for i in range(my_count)]
    plane_groups = [
        [(SIDE * x + y) * my_count + 2 * plane + one for plane in range(planes) for x in range(SIDE)]
        for y in range(SIDE)
        for one in range(2)
    ]

    below = [lax.ppermute(q_weight, "mx", shift_y(1))]
    above = [lax.ppermute(q_weight, "mx", shift_y(-1))]
    tokens, below[0], above[0] = lax.optimization_barrier((tokens, below[0], above[0]))
    copies = jnp.broadcast_to(tokens, (SIDE, *tokens.shape))
    gathered = lax.all_to_all(
        copies, "mx", split_axis=0, concat_axis=0, axis_index_groups=x_rings
    ).reshape(-1, width)
    for _ in range(2):
        below.append(lax.ppermute(below[-1], "mx", shift_y(1)))
        above.append(lax.ppermute(above[-1], "mx", shift_y(-1)))
    half = columns // 2
    opposite = (
        lax.ppermute(below[2][:, :half], "mx", shift_y(1)),
        lax.ppermute(above[2][:, half:], "mx", shift_y(-1)),
    )
    pair_columns = kv_weight.shape[1] // SIDE
    pair_weight = lax.dynamic_slice_in_dim(kv_weight, x_index * pair_columns, pair_columns, 1)

    def chip_sums(other_sums, same_sums):
        swapped = lax.ppermute(other_sums, "my", core_pairs)
        return (same_sums + swapped).reshape(planes * SIDE, -1, other_sums.shape[1])

    def exchange(sums):
        parts = lax.all_to_all(
            sums, ("mx", "my"), split_axis=0, concat_axis=0, axis_index_groups=plane_groups
        )
        sums = jnp.sum(parts.reshape(planes, SIDE, *parts.shape[1:]), axis=0)
        return sums.astype(jnp.bfloat16).reshape(SIDE, own_rows, -1)

    near = below[0], q_weight, above[0], above[1], below[1], pair_weight
    far = above[2], *opposite, below[2]
    near, far = (
        chip_sums(*strip_sums(planes, own_rows, core, gathered, *(piece.T for piece in pieces)))
        for pieces in (near, far)
    )
    far_at = near.shape[2]
    strip = exchange(jnp.concatenate([near, far], axis=2)).transpose(1, 0, 2)
    new_pairs = strip[:, :, 5 * columns : 5 * columns + pair_columns].reshape(own_rows, -1)
    query_rows = jnp.concatenate(
        [
            strip[:, :, : 4 * columns],
            strip[:, :, far_at : far_at + 3 * columns],
            strip[:, :, 4 * columns : 5 * columns],
        ],
        axis=2,
    )
    query_rows = query_rows.reshape(own_rows, SIDE, SIDE, columns)
    query_rows = jnp.concatenate([query_rows, query_rows], axis=2)
    query_rows = lax.dynamic_slice_in_dim(query_rows, (SIDE + 1 - y_index) % SIDE, SIDE, 2)
    queries = query_rows.reshape(own_rows, -1, head_size)

    return attend(lengths, queries, new_pairs, key_cache, value_cache).reshape(own_rows, -1)


def solution(mesh):
    return jax.shard_map(
        local,
        mesh=mesh,
        in_specs=(
            P("mx", "my"),
            P("my", "mx"),
            P("my", None),
            P(("mx", "my"), None, None),
            P(("mx", "my"), None, None),
            P(("mx", "my")),
        ),
        out_specs=P(("mx", "my"), None),
        check_vma=False,
    )
```
